32 devices in a mesh: groups: 2 (over y), block: 4 (over x, core), tensor: 4 (over z).
Axes of the slice: x: 2, y: 2, z: 4, core: 2. Of those that a mesh axis runs over, the one named last changes fastest.
Arguments:
- tokens: bfloat16 [4096, 5120], P(('groups', 'block', 'tensor')), parts along dimension 0, may hold values from -20 to 20
- mod_shift: float32 [5120], replicated, may hold values from -3 to 3
- mod_scale: float32 [5120], replicated, may hold values from -0.5 to 0.5
- w_qkv: bfloat16 [3, 5120, 1024], P(None, 'block', 'tensor'), may hold values from -1 to 1
- tile_list: int32 [8, 4, 5], P(('groups', 'block')), parts along dimension 0, may hold values from 0 to 7, as said below
- tile_count: int32 [8, 4], P(('groups', 'block')), parts along dimension 0, may hold values from 2 to 5, as said below
Outputs:
- attended: bfloat16 [4096, 1024], P(('groups', 'block'), 'tensor'), parts along dimension 0
The draws below stay inside these ranges and needn't reach their ends.
There are 2 independent parts, one for each index of `groups`. The reference program is written for one: setup_inputs(seed, part) draws one part's arguments, and reference() takes and returns one part's arrays. A program takes and returns all parts, laid end to end along the dimension named above; an argument that names none is the same for every part. Nothing has to cross between parts.
Inputs may be any that keep to these rules, and one draw needn't show every extreme that they name: `tile_list`: within the first tile_count[c, t] slots the entries are distinct, the first is the query tile itself (2 + t), and none names a tile outside the slab; blocks at scene cuts name no tile of the block across the cut. Later slots hold indices in range and are not read. `tile_count`: the first query tile of every block reads 5 slots.
All inputs are finite; a program needn't handle non-finite values.
Results may differ from the reference program's by a relative error of at most 0.0087.
Values may be sent and summed in bfloat16 or wider, within the bound.
A program may use at most 64 MiB of HBM per device.

```python
import jax
import jax.numpy as jnp
from jax import lax

D = 5120
HEAD_DIM = 128
BLOCK_TOK = 512
TILE = 128
BT = 2
KT = 5
HD = 1024
BLOCKS = 4
TOKENS = 2048
TPC = 4
NC = 8


def draw_tokens(key, part):
    first_key = jax.random.fold_in(key, 1)
    base = jax.random.normal(first_key, (TOKENS, D), jnp.float32)
    return jnp.clip(base, -20.0, 20.0).astype(jnp.bfloat16)


def draw_w_qkv(key, part):
    fan_scale = D ** (-0.5)
    noise = jax.random.normal(jax.random.fold_in(key, 5), (3, D, HD), jnp.float32) * fan_scale
    factors = jnp.array([1.5, 1.5, 1.0], jnp.float32)
    result = noise * factors[:, None, None]
    return jnp.clip(result, -1.0, 1.0).astype(jnp.bfloat16)


def tile_plan(key):
    cut_key = jax.random.fold_in(key, 11)
    score_key = jax.random.fold_in(key, 12)
    count_key = jax.random.fold_in(key, 13)
    block_ids = jnp.arange(BLOCKS, dtype=jnp.int32)
    cut_bits = jax.random.randint(cut_key, (BLOCKS,), 0, 2)
    cut_before = (cut_bits == 1) & (block_ids % 2 == 0) & (block_ids >= 2)
    cut_after = jnp.concatenate([cut_before[1:], jnp.zeros((1,), bool)])
    no_prev = (block_ids == 0) | cut_before
    no_next = (block_ids == BLOCKS - 1) | cut_after
    candidate = jnp.arange(NC, dtype=jnp.int32)
    valid = jnp.logical_not((candidate[None, :] < BT) & no_prev[:, None])
    valid = valid & jnp.logical_not((candidate[None, :] >= BT + TPC) & no_next[:, None])
    raw_scores = jax.random.randint(score_key, (BLOCKS, TPC, NC), 0, 1 << 20) * NC + candidate[None, None, :]
    own_tile = candidate[None, :] == (BT + jnp.arange(TPC, dtype=jnp.int32))[:, None]
    ranked = raw_scores + jnp.where(valid[:, None, :], 1 << 26, 0) + jnp.where(own_tile[None, :, :], 1 << 28, 0)
    unused, picked = lax.top_k(ranked, KT)
    counts = jax.random.randint(count_key, (BLOCKS, TPC), 2, KT + 1)
    tile_ids = jnp.arange(TPC, dtype=jnp.int32)[None, :]
    counts = jnp.where(tile_ids == 0, KT, counts)
    return (picked.astype(jnp.int32), counts.astype(jnp.int32))


def draw_tile_list(key, part):
    return tile_plan(key)[0]


def draw_tile_count(key, part):
    return tile_plan(key)[1]


def normal_values(stream_key, shape, deviation, most, kind=jnp.bfloat16):
    return jnp.clip(deviation * jax.random.normal(stream_key, shape, jnp.float32), -most, most).astype(kind)


def setup_inputs(seed: int = 0, part: int = 0) -> dict:
    key_of = jax.random.split(jax.random.key(seed), 7)
    part_keys = jax.random.split(jax.random.fold_in(key_of[6], part), 7)
    tokens = draw_tokens(jax.random.fold_in(jax.random.fold_in(key_of[6], part), 71), part)
    mod_shift = normal_values(key_of[1], (D,), 0.5, 3.0, jnp.float32)
    mod_scale = jnp.clip(jax.random.uniform(key_of[2], (D,), jnp.float32, -0.5, 0.5), -0.5, 0.5)
    w_qkv = draw_w_qkv(jax.random.fold_in(key_of[6], 71), part)
    tile_list = draw_tile_list(jax.random.fold_in(jax.random.fold_in(key_of[6], part), 71), part)
    tile_count = draw_tile_count(jax.random.fold_in(jax.random.fold_in(key_of[6], part), 71), part)
    return dict(tokens=tokens, mod_shift=mod_shift, mod_scale=mod_scale, w_qkv=w_qkv, tile_list=tile_list, tile_count=tile_count)


epsilon = 1e-06

def attend(queries, key_rows, value_rows, chosen_list, chosen_count):
    head_count = queries.shape[1] // HEAD_DIM
    local_tiles = queries.shape[0] // TILE
    all_tiles = key_rows.shape[0] // TILE
    slot_count = chosen_list.shape[1]
    shaped_queries = queries.reshape(local_tiles, TILE, head_count, HEAD_DIM).astype(jnp.float32)
    key_tiles = key_rows.reshape(all_tiles, TILE, head_count, HEAD_DIM)[chosen_list].astype(jnp.float32)
    value_tiles = value_rows.reshape(all_tiles, TILE, head_count, HEAD_DIM)[chosen_list].astype(jnp.float32)
    scores = jnp.einsum('pthd,pkshd->phtks', shaped_queries, key_tiles) * HEAD_DIM ** (-0.5)
    live_slot = jnp.arange(slot_count, dtype=jnp.int32)[None, :] < chosen_count[:, None]
    scores = jnp.where(live_slot[:, None, None, :, None], scores, jnp.float32(-1e+30))
    highest = lax.optimization_barrier(jnp.max(scores, axis=(3, 4), keepdims=True))
    exponent = jnp.exp(scores - highest)
    denominator = lax.optimization_barrier(jnp.sum(exponent, axis=(3, 4), keepdims=True))
    attn_weights = (exponent / denominator).astype(jnp.bfloat16)
    mixed = jnp.einsum('phtks,pkshd->pthd', attn_weights.astype(jnp.float32), value_tiles)
    return mixed.astype(jnp.bfloat16).reshape(local_tiles * TILE, head_count * HEAD_DIM)

def reference(tokens, mod_shift, mod_scale, w_qkv, tile_list, tile_count):
    values_in = tokens.astype(jnp.float32)
    row_mean = lax.optimization_barrier(jnp.mean(values_in, axis=1, keepdims=True))
    centred = values_in - row_mean
    row_var = lax.optimization_barrier(jnp.mean(centred * centred, axis=1, keepdims=True))
    normed = (centred * lax.rsqrt(row_var + epsilon) * (1.0 + mod_scale) + mod_shift).astype(jnp.bfloat16)
    queries = jnp.dot(normed, w_qkv[0], preferred_element_type=jnp.float32).astype(jnp.bfloat16)
    keys_all = jnp.dot(normed, w_qkv[1], preferred_element_type=jnp.float32).astype(jnp.bfloat16)
    values_all = jnp.dot(normed, w_qkv[2], preferred_element_type=jnp.float32).astype(jnp.bfloat16)
    margin = BT * TILE
    padding = jnp.zeros((margin, HD), jnp.bfloat16)
    keys_padded = jnp.concatenate([padding, keys_all, padding], axis=0)
    values_padded = jnp.concatenate([padding, values_all, padding], axis=0)

    def one_part(block_id):
        offset = (block_id * BLOCK_TOK).astype(jnp.int32)
        key_rows = lax.dynamic_slice_in_dim(keys_padded, offset, BLOCK_TOK + 2 * margin, 0)
        value_rows = lax.dynamic_slice_in_dim(values_padded, offset, BLOCK_TOK + 2 * margin, 0)
        own_queries = lax.dynamic_slice_in_dim(queries, offset, BLOCK_TOK, 0)
        return attend(own_queries, key_rows, value_rows, tile_list[block_id], tile_count[block_id])
    outputs = lax.map(one_part, jnp.arange(BLOCKS, dtype=jnp.int32))
    return outputs.reshape(TOKENS, HD)
```

```python
import functools

import jax
import jax.numpy as jnp
from jax import lax
from jax.experimental import pallas as pl
from jax.experimental.pallas import tpu as pltpu
from jax.sharding import PartitionSpec as P

HEAD_DIM = 128
TILE = 128
BT = 2
MARGIN = BT * TILE
CHUNK = 32
MESH = pl.DeviceIdType.MESH

epsilon = 1e-06


def project_kernel(
    nb, nt, tokens_ref, shift_ref, scale_ref, w_ref, q_ref, kv_ref,
    xg, wfull, qkvx, up_s, up_r, dn_s, dn_r, wx_s, wx_r, wp_s, wp_r, wl_s, hu_s, hu_r, hd_s, hd_r,
):
    g = lax.axis_index("groups")
    b = lax.axis_index("block")
    t = lax.axis_index("tensor")
    rows, _ = tokens_ref.shape
    kb = w_ref.shape[1]
    nc = rows // CHUNK
    total = rows * nt
    chips = nb // 2
    chip = b // 2
    core = b % 2
    partner = (g, chip * 2 + (1 - core), t)

    barrier = pltpu.get_barrier_semaphore()
    for j in range(1, nb):
        pl.semaphore_signal(barrier, inc=1, device_id=(g, (b + j) % nb, t), device_id_type=MESH)

    @pl.when(t > 0)
    def _():
        pl.semaphore_signal(barrier, inc=1, device_id=(g, b, t - 1), device_id_type=MESH)

    @pl.when(t < nt - 1)
    def _():
        pl.semaphore_signal(barrier, inc=1, device_id=(g, b, t + 1), device_id_type=MESH)

    ends = jnp.where(t == 0, 1, 0) + jnp.where(t == nt - 1, 1, 0)
    pl.semaphore_wait(barrier, nb + 1 - ends)

    def remote(src, dst, s, r, device):
        return pltpu.make_async_remote_copy(
            src_ref=src, dst_ref=dst, send_sem=s, recv_sem=r, device_id=device, device_id_type=MESH
        )

    def w_slab(owner, i):
        return wfull.at[i, pl.ds(pl.multiple_of(owner * kb, 16), kb)]

    def w_cross(j, i, owner, device):
        return remote(w_ref.at[i], w_slab(owner, i), wx_s.at[j, i], wx_r.at[j, i], device)

    def w_pair(j, i, src, owner):
        return remote(src, w_slab(owner, i), wp_s.at[j, i], wp_r.at[j, i], partner)

    for i in range(3):
        for j in range(1, chips):
            w_cross(j, i, b, (g, ((chip + j) % chips) * 2 + core, t)).start()
        w_pair(0, i, w_ref.at[i], b).start()
        pltpu.make_async_copy(w_ref.at[i], w_slab(b, i), wl_s.at[i]).start()

    def x_slab(o, c):
        return xg.at[pl.ds(pl.multiple_of(o * rows + c * CHUNK, 16), CHUNK)]

    def up(s, c):
        slab = x_slab(t - s, c)
        return remote(slab, slab, up_s.at[s, c], up_r.at[s, c], (g, b, t + 1))

    def down(s, c):
        slab = x_slab(t + s, c)
        return remote(slab, slab, dn_s.at[s, c], dn_r.at[s, c], (g, b, t - 1))

    def from_left(s, c):
        slab = x_slab(t - s, c)
        return remote(slab, slab, up_s.at[s - 1, c], up_r.at[s - 1, c], (g, b, t + 1))

    def from_right(s, c):
        slab = x_slab(t + s, c)
        return remote(slab, slab, dn_s.at[s - 1, c], dn_r.at[s - 1, c], (g, b, t - 1))

    gain = 1.0 + scale_ref[...]

    def norm(c, carry):
        x = tokens_ref[pl.ds(pl.multiple_of(c * CHUNK, 16), CHUNK), :].astype(jnp.float32)
        mean = jnp.mean(x, axis=1, keepdims=True)
        x = x - mean
        var = jnp.mean(x * x, axis=1, keepdims=True)
        y = x * lax.rsqrt(var + epsilon) * gain + shift_ref[...]
        xg[pl.ds(pl.multiple_of(t * rows + c * CHUNK, 16), CHUNK), :] = y.astype(jnp.bfloat16)

        @pl.when(t < nt - 1)
        def _():
            up(0, c).start()

        @pl.when(t > 0)
        def _():
            down(0, c).start()

        return carry

    lax.fori_loop(0, nc, norm, 0)

    zeros = jnp.zeros((2, MARGIN, qkvx.shape[2]), qkvx.dtype)

    @pl.when(b == 0)
    def _():
        qkvx[1:3, 0:MARGIN, :] = zeros

    @pl.when(b == nb - 1)
    def _():
        qkvx[1:3, MARGIN + total : 2 * MARGIN + total, :] = zeros

    def relay(s):
        def body(c, carry):
            @pl.when(t - s >= 0)
            def _():
                from_left(s, c).wait_recv()

                @pl.when(t < nt - 1)
                def _():
                    up(s, c).start()

            @pl.when(t + s < nt)
            def _():
                from_right(s, c).wait_recv()

                @pl.when(t > 0)
                def _():
                    down(s, c).start()

            return carry

        lax.fori_loop(0, nc, body, 0)

    def halo_up(o):
        return remote(
            qkvx.at[1:3, pl.ds(pl.multiple_of(MARGIN + o * rows, 16), rows)],
            qkvx.at[1:3, pl.ds(pl.multiple_of(o * rows - (total - MARGIN), 16), rows)],
            hu_s.at[o], hu_r.at[o], (g, b + 1, t),
        )

    def halo_down(o):
        return remote(
            qkvx.at[1:3, pl.ds(pl.multiple_of(MARGIN + o * rows, 16), rows)],
            qkvx.at[1:3, pl.ds(pl.multiple_of(MARGIN + total + o * rows, 16), rows)],
            hd_s.at[o], hd_r.at[o], (g, b - 1, t),
        )

    def project(o):
        x = xg[pl.ds(pl.multiple_of(o * rows, 16), rows), :]

        def one(i, carry):
            y = jnp.dot(x, wfull[i], preferred_element_type=jnp.float32)
            qkvx[i, pl.ds(pl.multiple_of(MARGIN + o * rows, 16), rows), :] = y.astype(jnp.bfloat16)
            return carry

        lax.fori_loop(0, 3, one, 0)

        @pl.when(jnp.logical_and(o * rows >= total - MARGIN, b < nb - 1))
        def _():
            halo_up(o).start()

        @pl.when(jnp.logical_and(o * rows < MARGIN, b > 0))
        def _():
            halo_down(o).start()

    relay(1)

    for i in range(3):
        for j in range(1, chips):
            owner = ((chip - j + chips) % chips) * 2 + core
            w_cross(j, i, owner, partner).wait_recv()
            w_pair(j, i, w_slab(owner, i), owner).start()
    for i in range(3):
        pltpu.make_async_copy(w_ref.at[i], w_slab(b, i), wl_s.at[i]).wait()
        for j in range(chips):
            owner = ((chip - j + chips) % chips) * 2 + (1 - core)
            w_pair(j, i, w_slab(owner, i), owner).wait_recv()

    project(t)

    def step(s, carry):
        @pl.when(s > 1)
        def _():
            relay(s)

        def side(d, carry):
            o = t + s * (2 * d - 1)

            @pl.when(jnp.logical_and(o >= 0, o < nt))
            def _():
                project(o)

            return carry

        lax.fori_loop(0, 2, side, 0)
        return carry

    lax.fori_loop(1, nt, step, 0)

    def drain(s, carry):
        def body(c, carry):
            @pl.when(jnp.logical_and(t - s >= 0, t < nt - 1))
            def _():
                up(s, c).wait_send()

            @pl.when(jnp.logical_and(t + s < nt, t > 0))
            def _():
                down(s, c).wait_send()

            return carry

        return lax.fori_loop(0, nc, body, carry)

    lax.fori_loop(0, nt, drain, 0)
    for i in range(3):
        for j in range(1, chips):
            w_cross(j, i, b, partner).wait_send()
        for j in range(chips):
            w_pair(j, i, w_ref.at[i], b).wait_send()

    q_ref[...] = qkvx[0, MARGIN : MARGIN + total, :]

    def halo_wait(o, carry):
        @pl.when(o * rows >= total - MARGIN)
        def _():
            @pl.when(b < nb - 1)
            def _():
                halo_up(o).wait_send()

            @pl.when(b > 0)
            def _():
                halo_up(o).wait_recv()

        @pl.when(o * rows < MARGIN)
        def _():
            @pl.when(b > 0)
            def _():
                halo_down(o).wait_send()

            @pl.when(b < nb - 1)
            def _():
                halo_down(o).wait_recv()

        return carry

    lax.fori_loop(0, nt, halo_wait, 0)
    kv_ref[...] = qkvx[1:3]


def attend_kernel(list_ref, count_ref, q_ref, kv_ref, out_ref):
    tiles = q_ref.shape[0] // TILE
    heads = q_ref.shape[1] // HEAD_DIM
    slots = list_ref.shape[2]
    for p in range(tiles):
        count = count_ref[0, p]
        starts = [pl.multiple_of(list_ref[0, p, s] * TILE, TILE) for s in range(slots)]
        for h in range(heads):
            cols = slice(h * HEAD_DIM, (h + 1) * HEAD_DIM)
            q = q_ref[p * TILE : (p + 1) * TILE, cols]
            keys = jnp.concatenate([kv_ref[0, pl.ds(a, TILE), cols] for a in starts], axis=0)
            vals = jnp.concatenate([kv_ref[1, pl.ds(a, TILE), cols] for a in starts], axis=0)
            scores = lax.dot_general(
                q, keys, (((1,), (1,)), ((), ())), preferred_element_type=jnp.float32
            ) * HEAD_DIM ** (-0.5)
            slot = lax.broadcasted_iota(jnp.int32, scores.shape, 1) // TILE
            scores = jnp.where(slot < count, scores, jnp.float32(-1e30))
            e = jnp.exp(scores - jnp.max(scores, axis=1, keepdims=True))
            weights = (e / jnp.sum(e, axis=1, keepdims=True)).astype(jnp.bfloat16)
            mixed = jnp.dot(weights, vals, preferred_element_type=jnp.float32)
            out_ref[p * TILE : (p + 1) * TILE, cols] = mixed.astype(jnp.bfloat16)


def shards(nb, nt, tokens, mod_shift, mod_scale, w_qkv, tile_list, tile_count):
    rows, d = tokens.shape
    width = w_qkv.shape[2]
    total = rows * nt
    nc = rows // CHUNK
    chips = nb // 2
    vmem = pl.BlockSpec(memory_space=pltpu.VMEM)
    smem = pl.BlockSpec(memory_space=pltpu.SMEM)
    dma = pltpu.SemaphoreType.DMA
    bf16 = jnp.bfloat16
    q, kv = pl.pallas_call(
        functools.partial(project_kernel, nb, nt),
        out_shape=(
            jax.ShapeDtypeStruct((total, width), bf16),
            jax.ShapeDtypeStruct((2, total + 2 * MARGIN, width), bf16),
        ),
        in_specs=[vmem, vmem, vmem, pl.BlockSpec(memory_space=pl.ANY)],
        out_specs=(vmem, vmem),
        scratch_shapes=[
            pltpu.VMEM((total, d), bf16),
            pltpu.VMEM((3, d, width), bf16),
            pltpu.VMEM((3, total + 2 * MARGIN, width), bf16),
            dma((nt, nc)), dma((nt, nc)), dma((nt, nc)), dma((nt, nc)),
            dma((chips, 3)), dma((chips, 3)), dma((chips, 3)), dma((chips, 3)), dma((3,)),
            dma((nt,)), dma((nt,)), dma((nt,)), dma((nt,)),
        ],
        compiler_params=pltpu.CompilerParams(
            collective_id=0, has_side_effects=True, vmem_limit_bytes=40 * 2**20
        ),
    )(tokens, mod_shift.reshape(1, d), mod_scale.reshape(1, d), w_qkv)
    return pl.pallas_call(
        attend_kernel,
        out_shape=jax.ShapeDtypeStruct((total, width), bf16),
        in_specs=[smem, smem, vmem, vmem],
        out_specs=vmem,
        compiler_params=pltpu.CompilerParams(vmem_limit_bytes=32 * 2**20),
    )(tile_list, tile_count, q, kv)


def solution(mesh):
    return jax.shard_map(
        functools.partial(shards, mesh.shape["block"], mesh.shape["tensor"]),
        mesh=mesh,
        in_specs=(
            P(("groups", "block", "tensor"), None),
            P(),
            P(),
            P(None, "block", "tensor"),
            P(("groups", "block"), None, None),
            P(("groups", "block"), None),
        ),
        out_specs=P(("groups", "block"), "tensor"),
        check_vma=False,
    )
```

```python
import functools

import jax
import jax.numpy as jnp
from jax import lax
from jax.experimental import pallas as pl
from jax.experimental.pallas import tpu as pltpu
from jax.sharding import PartitionSpec as P

HEAD_DIM = 128
TILE = 128
BT = 2
MARGIN = BT * TILE
CHUNK = 32
MESH = pl.DeviceIdType.MESH

epsilon = 1e-06


def project_kernel(
    helped, nb, nt, tokens_hbm, shift_ref, scale_ref, w_ref, q_ref, kv_ref,
    tokens_ref, xg, wfull, qkvx, wh, part_out, part_in, up_s, up_r, dn_s, dn_r, wx_s, wx_r, wp_s, wp_r, wl_s,
    hu_s, hu_r, hd_s, hd_r, hz_s, hz_r, hy_s, hy_r, hp_s, hp_r, pt_s, pt_r, tk_s,
):
    tokens_copy = pltpu.make_async_copy(tokens_hbm, tokens_ref, tk_s)
    tokens_copy.start()
    g = lax.axis_index("groups")
    b = lax.axis_index("block")
    t = lax.axis_index("tensor")
    rows, _ = tokens_ref.shape
    kb = w_ref.shape[1]
    nc = rows // CHUNK
    total = rows * nt
    chips = nb // 2
    chip = b // 2
    core = b % 2
    partner = (g, chip * 2 + (1 - core), t)
    lower = t < nt // 2
    sgn = jnp.where(lower, -1, 1)
    is_end = jnp.logical_or(t == 0, t == nt - 1)
    kc = 2 * kb

    barrier = pltpu.get_barrier_semaphore()
    for j in range(1, nb):
        pl.semaphore_signal(barrier, inc=1, device_id=(g, (b + j) % nb, t), device_id_type=MESH)

    @pl.when(t > 0)
    def _():
        pl.semaphore_signal(barrier, inc=1, device_id=(g, b, t - 1), device_id_type=MESH)

    @pl.when(t < nt - 1)
    def _():
        pl.semaphore_signal(barrier, inc=1, device_id=(g, b, t + 1), device_id_type=MESH)

    if helped:
        pl.semaphore_signal(barrier, inc=1, device_id=(1 - g, b, t), device_id_type=MESH)
    ends = jnp.where(t == 0, 1, 0) + jnp.where(t == nt - 1, 1, 0)
    pl.semaphore_wait(barrier, nb + 1 - ends + (1 if helped else 0))

    def remote(src, dst, s, r, device):
        return pltpu.make_async_remote_copy(
            src_ref=src, dst_ref=dst, send_sem=s, recv_sem=r, device_id=device, device_id_type=MESH
        )

    def w_slab(owner, i):
        return wfull.at[i, pl.ds(pl.multiple_of(owner * kb, 16), kb)]

    def w_cross(j, i, owner, device):
        return remote(w_ref.at[i], w_slab(owner, i), wx_s.at[j, i], wx_r.at[j, i], device)

    def w_pair(j, i, src, owner):
        return remote(src, w_slab(owner, i), wp_s.at[j, i], wp_r.at[j, i], partner)

    for i in range(3):
        for j in range(1, chips):
            w_cross(j, i, b, (g, ((chip + j) % chips) * 2 + core, t)).start()
        w_pair(0, i, w_ref.at[i], b).start()
        pltpu.make_async_copy(w_ref.at[i], w_slab(b, i), wl_s.at[i]).start()

    half = kb // 2

    def h_slab(i, c, part):
        return wh.at[i, pl.ds(pl.multiple_of(c * kb + part * half, 16), half)]

    def h_line(i):
        src = w_ref.at[i, pl.ds(pl.multiple_of(g * half, 16), half)]
        return remote(src, h_slab(i, core, g), hz_s.at[i], hz_r.at[i], (g, b, t - sgn))

    def h_group(i, part):
        slab = h_slab(i, core, part)
        return remote(slab, slab, hy_s.at[i], hy_r.at[i], (1 - g, b, t))

    def h_pair(i, k, c, part):
        slab = h_slab(i, c, part)
        return remote(slab, slab, hp_s.at[k, i], hp_r.at[k, i], partner)

    if helped:

        @pl.when(is_end)
        def _():
            for i in range(3):
                h_line(i).start()

    def x_slab(o, c):
        return xg.at[pl.ds(pl.multiple_of(o * rows + c * CHUNK, 16), CHUNK)]

    def x_half(o, c):
        return xg.at[
            pl.ds(pl.multiple_of(o * rows + c * CHUNK, 16), CHUNK), pl.ds(pl.multiple_of((1 - chip) * kc, 128), kc)
        ]

    def up(s, c, slab=x_slab):
        slab = slab(t - s, c)
        return remote(slab, slab, up_s.at[s, c], up_r.at[s, c], (g, b, t + 1))

    def down(s, c, slab=x_slab):
        slab = slab(t + s, c)
        return remote(slab, slab, dn_s.at[s, c], dn_r.at[s, c], (g, b, t - 1))

    def from_left(s, c, slab=x_slab):
        slab = slab(t - s, c)
        return remote(slab, slab, up_s.at[s - 1, c], up_r.at[s - 1, c], (g, b, t + 1))

    def from_right(s, c, slab=x_slab):
        slab = slab(t + s, c)
        return remote(slab, slab, dn_s.at[s - 1, c], dn_r.at[s - 1, c], (g, b, t - 1))

    def by_width(narrow, act):
        if not helped:
            act(x_slab)
            return

        @pl.when(narrow)
        def _():
            act(x_half)

        @pl.when(jnp.logical_not(narrow))
        def _():
            act(x_slab)

    gain = 1.0 + scale_ref[...]
    tokens_copy.wait()

    def norm(c, carry):
        x = tokens_ref[pl.ds(pl.multiple_of(c * CHUNK, 16), CHUNK), :].astype(jnp.float32)
        mean = jnp.mean(x, axis=1, keepdims=True)
        x = x - mean
        var = jnp.mean(x * x, axis=1, keepdims=True)
        y = x * lax.rsqrt(var + epsilon) * gain + shift_ref[...]
        xg[pl.ds(pl.multiple_of(t * rows + c * CHUNK, 16), CHUNK), :] = y.astype(jnp.bfloat16)

        @pl.when(t < nt - 1)
        def _():
            up(0, c).start()

        @pl.when(t > 0)
        def _():
            down(0, c).start()

        return carry

    lax.fori_loop(0, nc, norm, 0)

    zeros = jnp.zeros((2, MARGIN, qkvx.shape[2]), qkvx.dtype)

    @pl.when(b == 0)
    def _():
        qkvx[1:3, 0:MARGIN, :] = zeros

    @pl.when(b == nb - 1)
    def _():
        qkvx[1:3, MARGIN + total : 2 * MARGIN + total, :] = zeros

    def relay_left(s):
        @pl.when(t - s >= 0)
        def _():
            def body(c, carry):
                by_width(jnp.logical_and(t == nt - 1, s >= 2), lambda slab: from_left(s, c, slab).wait_recv())

                @pl.when(t < nt - 1)
                def _():
                    by_width(t == nt - 2, lambda slab: up(s, c, slab).start())

                return carry

            lax.fori_loop(0, nc, body, 0)

    def relay_right(s):
        @pl.when(t + s < nt)
        def _():
            def body(c, carry):
                by_width(jnp.logical_and(t == 0, s >= 2), lambda slab: from_right(s, c, slab).wait_recv())

                @pl.when(t > 0)
                def _():
                    by_width(t == 1, lambda slab: down(s, c, slab).start())

                return carry

            lax.fori_loop(0, nc, body, 0)

    def relay(s):
        relay_left(s)
        relay_right(s)

    def relay_far(s):
        @pl.when(lower)
        def _():
            relay_right(s)

        @pl.when(jnp.logical_not(lower))
        def _():
            relay_left(s)

    def relay_near(s):
        @pl.when(lower)
        def _():
            relay_left(s)

        @pl.when(jnp.logical_not(lower))
        def _():
            relay_right(s)

    def part_send(k):
        return remote(part_out.at[k], part_in.at[k], pt_s.at[k], pt_r.at[k], (g, b, t + sgn))

    def help_end(k):
        o = t - sgn * (k + 1)
        x = xg[pl.ds(pl.multiple_of(o * rows, 16), rows), pl.ds(pl.multiple_of(chip * kc, 128), kc)]

        def one(i, carry):
            y = jnp.dot(x, wh[i], preferred_element_type=jnp.float32)
            part_out[k, i] = y.astype(jnp.bfloat16)
            return carry

        lax.fori_loop(0, 3, one, 0)
        part_send(k).start()

    def halo_up(o):
        return remote(
            qkvx.at[1:3, pl.ds(pl.multiple_of(MARGIN + o * rows, 16), rows)],
            qkvx.at[1:3, pl.ds(pl.multiple_of(o * rows - (total - MARGIN), 16), rows)],
            hu_s.at[o], hu_r.at[o], (g, b + 1, t),
        )

    def halo_down(o):
        return remote(
            qkvx.at[1:3, pl.ds(pl.multiple_of(MARGIN + o * rows, 16), rows)],
            qkvx.at[1:3, pl.ds(pl.multiple_of(MARGIN + total + o * rows, 16), rows)],
            hd_s.at[o], hd_r.at[o], (g, b - 1, t),
        )

    def store(i, o, y):
        qkvx[i, pl.ds(pl.multiple_of(MARGIN + o * rows, 16), rows), :] = y.astype(jnp.bfloat16)

    def whole(o):
        x = xg[pl.ds(pl.multiple_of(o * rows, 16), rows), :]

        def one(i, carry):
            store(i, o, jnp.dot(x, wfull[i], preferred_element_type=jnp.float32))
            return carry

        lax.fori_loop(0, 3, one, 0)

    def rest(o, k):
        other = pl.ds(pl.multiple_of((1 - chip) * kc, 128), kc)
        x = xg[pl.ds(pl.multiple_of(o * rows, 16), rows), other]
        part_send(k).wait_recv()

        def one(i, carry):
            y = jnp.dot(x, wfull[i, other, :], preferred_element_type=jnp.float32)
            store(i, o, y + part_in[k, i].astype(jnp.float32))
            return carry

        lax.fori_loop(0, 3, one, 0)

    def project(o, s):
        if helped:
            narrow = jnp.logical_and(is_end, s >= 2)

            @pl.when(narrow)
            def _():
                rest(o, s - 2)

            @pl.when(jnp.logical_not(narrow))
            def _():
                whole(o)
        else:
            whole(o)

        @pl.when(jnp.logical_and(o * rows >= total - MARGIN, b < nb - 1))
        def _():
            halo_up(o).start()

        @pl.when(jnp.logical_and(o * rows < MARGIN, b > 0))
        def _():
            halo_down(o).start()

    if helped:
        relay_far(1)

        @pl.when(jnp.logical_not(is_end))
        def _():
            for i in range(3):
                h_line(i).wait_recv()
                h_group(i, g).start()
                h_pair(i, 0, core, g).start()

        relay_near(1)
    else:
        relay(1)

    for i in range(3):
        for j in range(1, chips):
            owner = ((chip - j + chips) % chips) * 2 + core
            w_cross(j, i, owner, partner).wait_recv()
            w_pair(j, i, w_slab(owner, i), owner).start()

    if helped:

        @pl.when(jnp.logical_not(is_end))
        def _():
            for i in range(3):
                h_group(i, 1 - g).wait_recv()
                h_pair(i, 1, core, 1 - g).start()

        relay_far(2)

        @pl.when(jnp.logical_not(is_end))
        def _():
            for i in range(3):
                h_pair(i, 0, 1 - core, g).wait_recv()
                h_pair(i, 1, 1 - core, 1 - g).wait_recv()

            def assist(k, carry):
                help_end(k)
                return carry

            lax.fori_loop(0, nt - 2, assist, 0)

    for i in range(3):
        pltpu.make_async_copy(w_ref.at[i], w_slab(b, i), wl_s.at[i]).wait()
        for j in range(chips):
            owner = ((chip - j + chips) % chips) * 2 + (1 - core)
            w_pair(j, i, w_slab(owner, i), owner).wait_recv()

    def step(s, carry):
        @pl.when(s > (2 if helped else 1))
        def _():
            relay(s)

        def side(d, carry):
            o = t + s * (2 * d - 1)

            @pl.when(jnp.logical_and(o >= 0, o < nt))
            def _():
                project(o, s)

            return carry

        lax.fori_loop(jnp.where(s == 0, 1, 0), 2, side, 0)
        return carry

    lax.fori_loop(0, nt, step, 0)

    def drain(s, carry):
        def body(c, carry):
            @pl.when(jnp.logical_and(t - s >= 0, t < nt - 1))
            def _():
                by_width(jnp.logical_and(t == nt - 2, s >= 1), lambda slab: up(s, c, slab).wait_send())

            @pl.when(jnp.logical_and(t + s < nt, t > 0))
            def _():
                by_width(jnp.logical_and(t == 1, s >= 1), lambda slab: down(s, c, slab).wait_send())

            return carry

        return lax.fori_loop(0, nc, body, carry)

    lax.fori_loop(0, nt, drain, 0)
    for i in range(3):
        for j in range(1, chips):
            w_cross(j, i, b, partner).wait_send()
        for j in range(chips):
            w_pair(j, i, w_ref.at[i], b).wait_send()

    if helped:

        @pl.when(is_end)
        def _():
            for i in range(3):
                h_line(i).wait_send()

        @pl.when(jnp.logical_not(is_end))
        def _():
            for i in range(3):
                h_group(i, g).wait_send()
                h_pair(i, 0, core, g).wait_send()
                h_pair(i, 1, core, 1 - g).wait_send()
            for k in range(nt - 2):
                part_send(k).wait_send()

    q_ref[...] = qkvx[0, MARGIN : MARGIN + total, :]

    def halo_wait(o, carry):
        @pl.when(o * rows >= total - MARGIN)
        def _():
            @pl.when(b < nb - 1)
            def _():
                halo_up(o).wait_send()

            @pl.when(b > 0)
            def _():
                halo_up(o).wait_recv()

        @pl.when(o * rows < MARGIN)
        def _():
            @pl.when(b > 0)
            def _():
                halo_down(o).wait_send()

            @pl.when(b < nb - 1)
            def _():
                halo_down(o).wait_recv()

        return carry

    lax.fori_loop(0, nt, halo_wait, 0)
    kv_ref[...] = qkvx[1:3]


def attend_kernel(list_ref, count_ref, q_ref, kv_ref, out_ref):
    tiles = q_ref.shape[0] // TILE
    heads = q_ref.shape[1] // HEAD_DIM
    slots = list_ref.shape[2]
    for p in range(tiles):
        count = count_ref[0, p]
        starts = [pl.multiple_of(list_ref[0, p, s] * TILE, TILE) for s in range(slots)]
        for h in range(heads):
            cols = slice(h * HEAD_DIM, (h + 1) * HEAD_DIM)
            q = q_ref[p * TILE : (p + 1) * TILE, cols]
            keys = jnp.concatenate([kv_ref[0, pl.ds(a, TILE), cols] for a in starts], axis=0)
            vals = jnp.concatenate([kv_ref[1, pl.ds(a, TILE), cols] for a in starts], axis=0)
            scores = lax.dot_general(
                q, keys, (((1,), (1,)), ((), ())), preferred_element_type=jnp.float32
            ) * HEAD_DIM ** (-0.5)
            slot = lax.broadcasted_iota(jnp.int32, scores.shape, 1) // TILE
            scores = jnp.where(slot < count, scores, jnp.float32(-1e30))
            e = jnp.exp(scores - jnp.max(scores, axis=1, keepdims=True))
            weights = (e / jnp.sum(e, axis=1, keepdims=True)).astype(jnp.bfloat16)
            mixed = jnp.dot(weights, vals, preferred_element_type=jnp.float32)
            out_ref[p * TILE : (p + 1) * TILE, cols] = mixed.astype(jnp.bfloat16)


def shards(ng, nb, nt, tokens, mod_shift, mod_scale, w_qkv, tile_list, tile_count):
    rows, d = tokens.shape
    width = w_qkv.shape[2]
    total = rows * nt
    nc = rows // CHUNK
    chips = nb // 2
    kb = w_qkv.shape[1]
    helped = ng == 2 and chips == 2 and nt == 4 and kb % 64 == 0
    help_rows = 2 * kb if helped else 16
    slots = nt - 2 if helped else 1
    vmem = pl.BlockSpec(memory_space=pltpu.VMEM)
    smem = pl.BlockSpec(memory_space=pltpu.SMEM)
    dma = pltpu.SemaphoreType.DMA
    bf16 = jnp.bfloat16
    q, kv = pl.pallas_call(
        functools.partial(project_kernel, helped, nb, nt),
        out_shape=(
            jax.ShapeDtypeStruct((total, width), bf16),
            jax.ShapeDtypeStruct((2, total + 2 * MARGIN, width), bf16),
        ),
        in_specs=[pl.BlockSpec(memory_space=pl.ANY), vmem, vmem, pl.BlockSpec(memory_space=pl.ANY)],
        out_specs=(vmem, vmem),
        scratch_shapes=[
            pltpu.VMEM((rows, d), bf16),
            pltpu.VMEM((total, d), bf16),
            pltpu.VMEM((3, d, width), bf16),
            pltpu.VMEM((3, total + 2 * MARGIN, width), bf16),
            pltpu.VMEM((3, help_rows, width), bf16),
            pltpu.VMEM((slots, 3, rows, width), bf16),
            pltpu.VMEM((slots, 3, rows, width), bf16),
            dma((nt, nc)), dma((nt, nc)), dma((nt, nc)), dma((nt, nc)),
            dma((chips, 3)), dma((chips, 3)), dma((chips, 3)), dma((chips, 3)), dma((3,)),
            dma((nt,)), dma((nt,)), dma((nt,)), dma((nt,)),
            dma((3,)), dma((3,)), dma((3,)), dma((3,)), dma((2, 3)), dma((2, 3)), dma((slots,)), dma((slots,)), dma,
        ],
        compiler_params=pltpu.CompilerParams(
            collective_id=0, has_side_effects=True, vmem_limit_bytes=40 * 2**20
        ),
    )(tokens, mod_shift.reshape(1, d), mod_scale.reshape(1, d), w_qkv)
    return pl.pallas_call(
        attend_kernel,
        out_shape=jax.ShapeDtypeStruct((total, width), bf16),
        in_specs=[smem, smem, vmem, vmem],
        out_specs=vmem,
        compiler_params=pltpu.CompilerParams(vmem_limit_bytes=32 * 2**20),
    )(tile_list, tile_count, q, kv)


def solution(mesh):
    return jax.shard_map(
        functools.partial(shards, mesh.shape["groups"], mesh.shape["block"], mesh.shape["tensor"]),
        mesh=mesh,
        in_specs=(
            P(("groups", "block", "tensor"), None),
            P(),
            P(),
            P(None, "block", "tensor"),
            P(("groups", "block"), None, None),
            P(("groups", "block"), None),
        ),
        out_specs=P(("groups", "block"), "tensor"),
        check_vma=False,
    )
```

```python
import functools

import jax
import jax.numpy as jnp
from jax import lax
from jax.experimental import pallas as pl
from jax.experimental.pallas import tpu as pltpu
from jax.sharding import PartitionSpec as P

HEAD_DIM = 128
TILE = 128
BT = 2
MARGIN = BT * TILE
CHUNK = 32
MESH = pl.DeviceIdType.MESH

epsilon = 1e-06


def project_kernel(
    helped, nb, nt, tokens_hbm, shift_hbm, scale_hbm, w_ref, q_ref, kv_ref,
    tokens_ref, shift_ref, scale_ref, xg, wfull, qkvx, wh, part_out, part_in, up_s, up_r, dn_s, dn_r, wx_s, wx_r, wp_s, wp_r, wl_s,
    hu_s, hu_r, hd_s, hd_r, hz_s, hz_r, hy_s, hy_r, hp_s, hp_r, pt_s, pt_r, tk_s, sh_s, sc_s,
):
    tokens_copy = pltpu.make_async_copy(tokens_hbm, tokens_ref, tk_s)
    tokens_copy.start()
    shift_copy = pltpu.make_async_copy(shift_hbm, shift_ref, sh_s)
    shift_copy.start()
    scale_copy = pltpu.make_async_copy(scale_hbm, scale_ref, sc_s)
    scale_copy.start()
    g = lax.axis_index("groups")
    b = lax.axis_index("block")
    t = lax.axis_index("tensor")
    rows, _ = tokens_ref.shape
    kb = w_ref.shape[1]
    nc = rows // CHUNK
    total = rows * nt
    chips = nb // 2
    chip = b // 2
    core = b % 2
    partner = (g, chip * 2 + (1 - core), t)
    lower = t < nt // 2
    sgn = jnp.where(lower, -1, 1)
    is_end = jnp.logical_or(t == 0, t == nt - 1)
    kc = 2 * kb

    barrier = pltpu.get_barrier_semaphore()
    for j in range(1, nb):
        pl.semaphore_signal(barrier, inc=1, device_id=(g, (b + j) % nb, t), device_id_type=MESH)

    @pl.when(t > 0)
    def _():
        pl.semaphore_signal(barrier, inc=1, device_id=(g, b, t - 1), device_id_type=MESH)

    @pl.when(t < nt - 1)
    def _():
        pl.semaphore_signal(barrier, inc=1, device_id=(g, b, t + 1), device_id_type=MESH)

    if helped:
        pl.semaphore_signal(barrier, inc=1, device_id=(1 - g, b, t), device_id_type=MESH)
    ends = jnp.where(t == 0, 1, 0) + jnp.where(t == nt - 1, 1, 0)
    pl.semaphore_wait(barrier, nb + 1 - ends + (1 if helped else 0))

    def remote(src, dst, s, r, device):
        return pltpu.make_async_remote_copy(
            src_ref=src, dst_ref=dst, send_sem=s, recv_sem=r, device_id=device, device_id_type=MESH
        )

    def w_slab(owner, i):
        return wfull.at[i, pl.ds(pl.multiple_of(owner * kb, 16), kb)]

    def w_cross(j, i, owner, device):
        return remote(w_ref.at[i], w_slab(owner, i), wx_s.at[j, i], wx_r.at[j, i], device)

    def w_pair(j, i, src, owner):
        return remote(src, w_slab(owner, i), wp_s.at[j, i], wp_r.at[j, i], partner)

    for i in range(3):
        for j in range(1, chips):
            w_cross(j, i, b, (g, ((chip + j) % chips) * 2 + core, t)).start()
        w_pair(0, i, w_ref.at[i], b).start()
        pltpu.make_async_copy(w_ref.at[i], w_slab(b, i), wl_s.at[i]).start()

    half = kb // 2

    def h_slab(i, c, part):
        return wh.at[i, pl.ds(pl.multiple_of(c * kb + part * half, 16), half)]

    def h_line(i):
        src = w_ref.at[i, pl.ds(pl.multiple_of(g * half, 16), half)]
        return remote(src, h_slab(i, core, g), hz_s.at[i], hz_r.at[i], (g, b, t - sgn))

    def h_group(i, part):
        slab = h_slab(i, core, part)
        return remote(slab, slab, hy_s.at[i], hy_r.at[i], (1 - g, b, t))

    def h_pair(i, k, c, part):
        slab = h_slab(i, c, part)
        return remote(slab, slab, hp_s.at[k, i], hp_r.at[k, i], partner)

    if helped:

        @pl.when(is_end)
        def _():
            for i in range(3):
                h_line(i).start()

    def x_slab(o, c):
        return xg.at[pl.ds(pl.multiple_of(o * rows + c * CHUNK, 16), CHUNK)]

    def x_half(o, c):
        return xg.at[
            pl.ds(pl.multiple_of(o * rows + c * CHUNK, 16), CHUNK), pl.ds(pl.multiple_of((1 - chip) * kc, 128), kc)
        ]

    def up(s, c, slab=x_slab):
        slab = slab(t - s, c)
        return remote(slab, slab, up_s.at[s, c], up_r.at[s, c], (g, b, t + 1))

    def down(s, c, slab=x_slab):
        slab = slab(t + s, c)
        return remote(slab, slab, dn_s.at[s, c], dn_r.at[s, c], (g, b, t - 1))

    def from_left(s, c, slab=x_slab):
        slab = slab(t - s, c)
        return remote(slab, slab, up_s.at[s - 1, c], up_r.at[s - 1, c], (g, b, t + 1))

    def from_right(s, c, slab=x_slab):
        slab = slab(t + s, c)
        return remote(slab, slab, dn_s.at[s - 1, c], dn_r.at[s - 1, c], (g, b, t - 1))

    def by_width(narrow, act):
        if not helped:
            act(x_slab)
            return

        @pl.when(narrow)
        def _():
            act(x_half)

        @pl.when(jnp.logical_not(narrow))
        def _():
            act(x_slab)

    scale_copy.wait()
    shift_copy.wait()
    tokens_copy.wait()
    gain = 1.0 + scale_ref[...]

    def norm(c, carry):
        x = tokens_ref[pl.ds(pl.multiple_of(c * CHUNK, 16), CHUNK), :].astype(jnp.float32)
        mean = jnp.mean(x, axis=1, keepdims=True)
        x = x - mean
        var = jnp.mean(x * x, axis=1, keepdims=True)
        y = x * lax.rsqrt(var + epsilon) * gain + shift_ref[...]
        xg[pl.ds(pl.multiple_of(t * rows + c * CHUNK, 16), CHUNK), :] = y.astype(jnp.bfloat16)

        @pl.when(t < nt - 1)
        def _():
            up(0, c).start()

        @pl.when(t > 0)
        def _():
            down(0, c).start()

        return carry

    if helped:

        @pl.when(is_end)
        def _():
            for i in range(3):
                h_line(i).wait_send()

    lax.fori_loop(0, nc, norm, 0)

    zeros = jnp.zeros((2, MARGIN, qkvx.shape[2]), qkvx.dtype)

    @pl.when(b == 0)
    def _():
        qkvx[1:3, 0:MARGIN, :] = zeros

    @pl.when(b == nb - 1)
    def _():
        qkvx[1:3, MARGIN + total : 2 * MARGIN + total, :] = zeros

    def relay_left(s, after=None):
        @pl.when(t - s >= 0)
        def _():
            def body(c, carry):
                by_width(jnp.logical_and(t == nt - 1, s >= 2), lambda slab: from_left(s, c, slab).wait_recv())

                @pl.when(t < nt - 1)
                def _():
                    by_width(t == nt - 2, lambda slab: up(s, c, slab).start())

                if after is not None:
                    after(c)
                return carry

            lax.fori_loop(0, nc, body, 0)

    def relay_right(s, after=None):
        @pl.when(t + s < nt)
        def _():
            def body(c, carry):
                by_width(jnp.logical_and(t == 0, s >= 2), lambda slab: from_right(s, c, slab).wait_recv())

                @pl.when(t > 0)
                def _():
                    by_width(t == 1, lambda slab: down(s, c, slab).start())

                if after is not None:
                    after(c)
                return carry

            lax.fori_loop(0, nc, body, 0)

    def relay(s):
        relay_left(s)
        relay_right(s)

    def relay_far(s, after=None):
        @pl.when(lower)
        def _():
            relay_right(s, after)

        @pl.when(jnp.logical_not(lower))
        def _():
            relay_left(s, after)

    def relay_near(s):
        @pl.when(lower)
        def _():
            relay_left(s)

        @pl.when(jnp.logical_not(lower))
        def _():
            relay_right(s)

    def part_send(k):
        return remote(part_out.at[k], part_in.at[k], pt_s.at[k], pt_r.at[k], (g, b, t + sgn))

    def help_end(k):
        o = t - sgn * (k + 1)
        x = xg[pl.ds(pl.multiple_of(o * rows, 16), rows), pl.ds(pl.multiple_of(chip * kc, 128), kc)]

        def one(i, carry):
            y = jnp.dot(x, wh[i], preferred_element_type=jnp.float32)
            part_out[k, i] = y.astype(jnp.bfloat16)
            return carry

        lax.fori_loop(0, 3, one, 0)
        part_send(k).start()

    def halo_up(o):
        return remote(
            qkvx.at[1:3, pl.ds(pl.multiple_of(MARGIN + o * rows, 16), rows)],
            qkvx.at[1:3, pl.ds(pl.multiple_of(o * rows - (total - MARGIN), 16), rows)],
            hu_s.at[o], hu_r.at[o], (g, b + 1, t),
        )

    def halo_down(o):
        return remote(
            qkvx.at[1:3, pl.ds(pl.multiple_of(MARGIN + o * rows, 16), rows)],
            qkvx.at[1:3, pl.ds(pl.multiple_of(MARGIN + total + o * rows, 16), rows)],
            hd_s.at[o], hd_r.at[o], (g, b - 1, t),
        )

    def store(i, o, y):
        qkvx[i, pl.ds(pl.multiple_of(MARGIN + o * rows, 16), rows), :] = y.astype(jnp.bfloat16)

    def whole(o):
        x = xg[pl.ds(pl.multiple_of(o * rows, 16), rows), :]

        def one(i, carry):
            store(i, o, jnp.dot(x, wfull[i], preferred_element_type=jnp.float32))
            return carry

        lax.fori_loop(0, 3, one, 0)

    def rest(o, k):
        other = pl.ds(pl.multiple_of((1 - chip) * kc, 128), kc)
        x = xg[pl.ds(pl.multiple_of(o * rows, 16), rows), other]
        part_send(k).wait_recv()

        def one(i, carry):
            y = jnp.dot(x, wfull[i, other, :], preferred_element_type=jnp.float32)
            store(i, o, y + part_in[k, i].astype(jnp.float32))
            return carry

        lax.fori_loop(0, 3, one, 0)

    def project(o, s):
        if helped:
            narrow = jnp.logical_and(is_end, s >= 2)

            @pl.when(narrow)
            def _():
                rest(o, s - 2)

            @pl.when(jnp.logical_not(narrow))
            def _():
                whole(o)
        else:
            whole(o)

        halos(o)

    def halos(o):
        @pl.when(jnp.logical_and(o * rows >= total - MARGIN, b < nb - 1))
        def _():
            halo_up(o).start()

        @pl.when(jnp.logical_and(o * rows < MARGIN, b > 0))
        def _():
            halo_down(o).start()

    if helped:

        @pl.when(jnp.logical_not(is_end))
        def _():
            for i in range(3):
                h_line(i).wait_recv()
                h_group(i, g).start()
                h_pair(i, 0, core, g).start()

        relay_far(1)
        relay_near(1)
    else:
        relay(1)

    for i in range(3):
        for j in range(1, chips):
            owner = ((chip - j + chips) % chips) * 2 + core
            w_cross(j, i, owner, partner).wait_recv()
            w_pair(j, i, w_slab(owner, i), owner).start()

    if helped:

        @pl.when(jnp.logical_not(is_end))
        def _():
            for i in range(3):
                h_group(i, 1 - g).wait_recv()
                h_pair(i, 1, core, 1 - g).start()

    for i in range(3):
        pltpu.make_async_copy(w_ref.at[i], w_slab(b, i), wl_s.at[i]).wait()
        for j in range(chips):
            owner = ((chip - j + chips) % chips) * 2 + (1 - core)
            w_pair(j, i, w_slab(owner, i), owner).wait_recv()

    if helped:
        each = -(-6 // nc)

        def between(c):
            def unit(u, carry):
                o = t - sgn * (u // 3)
                i = u % 3
                x = xg[pl.ds(pl.multiple_of(o * rows, 16), rows), :]
                store(i, o, jnp.dot(x, wfull[i], preferred_element_type=jnp.float32))
                return carry

            lax.fori_loop(jnp.minimum(each * c, 6), jnp.minimum(each * (c + 1), 6), unit, 0)

            @pl.when(jnp.logical_and(c == min(1, nc - 1), jnp.logical_not(is_end)))
            def _():
                for i in range(3):
                    h_pair(i, 0, 1 - core, g).wait_recv()
                    h_pair(i, 1, 1 - core, 1 - g).wait_recv()
                help_end(0)

        relay_far(2, between)

        @pl.when(jnp.logical_not(is_end))
        def _():
            def assist(k, carry):
                help_end(k)
                return carry

            lax.fori_loop(1, nt - 2, assist, 0)

        halos(t)
        halos(t - sgn)

    def step(s, carry):
        @pl.when(s > (2 if helped else 1))
        def _():
            relay(s)

        def side(d, carry):
            o = t + s * (2 * d - 1)
            todo = jnp.logical_and(o >= 0, o < nt)
            if helped:
                todo = jnp.logical_and(todo, o != t - sgn)

            @pl.when(todo)
            def _():
                project(o, s)

            return carry

        lax.fori_loop(jnp.where(s == 0, 1, 0), 2, side, 0)
        return carry

    lax.fori_loop(1 if helped else 0, nt, step, 0)

    def drain(s, carry):
        def body(c, carry):
            @pl.when(jnp.logical_and(t - s >= 0, t < nt - 1))
            def _():
                by_width(jnp.logical_and(t == nt - 2, s >= 1), lambda slab: up(s, c, slab).wait_send())

            @pl.when(jnp.logical_and(t + s < nt, t > 0))
            def _():
                by_width(jnp.logical_and(t == 1, s >= 1), lambda slab: down(s, c, slab).wait_send())

            return carry

        return lax.fori_loop(0, nc, body, carry)

    lax.fori_loop(0, nt, drain, 0)
    for i in range(3):
        for j in range(1, chips):
            w_cross(j, i, b, partner).wait_send()
        for j in range(chips):
            w_pair(j, i, w_ref.at[i], b).wait_send()

    if helped:

        @pl.when(jnp.logical_not(is_end))
        def _():
            for i in range(3):
                h_group(i, g).wait_send()
                h_pair(i, 0, core, g).wait_send()
                h_pair(i, 1, core, 1 - g).wait_send()
            for k in range(nt - 2):
                part_send(k).wait_send()

    q_ref[...] = qkvx[0, MARGIN : MARGIN + total, :]

    def halo_wait(o, carry):
        @pl.when(o * rows >= total - MARGIN)
        def _():
            @pl.when(b < nb - 1)
            def _():
                halo_up(o).wait_send()

            @pl.when(b > 0)
            def _():
                halo_up(o).wait_recv()

        @pl.when(o * rows < MARGIN)
        def _():
            @pl.when(b > 0)
            def _():
                halo_down(o).wait_send()

            @pl.when(b < nb - 1)
            def _():
                halo_down(o).wait_recv()

        return carry

    lax.fori_loop(0, nt, halo_wait, 0)
    kv_ref[...] = qkvx[1:3]


def attend_kernel(list_ref, count_ref, q_ref, kv_ref, out_ref):
    tiles = q_ref.shape[0] // TILE
    heads = q_ref.shape[1] // HEAD_DIM
    slots = list_ref.shape[2]
    for p in range(tiles):
        count = count_ref[0, p]
        starts = [pl.multiple_of(list_ref[0, p, s] * TILE, TILE) for s in range(slots)]
        for h in range(heads):
            cols = slice(h * HEAD_DIM, (h + 1) * HEAD_DIM)
            q = q_ref[p * TILE : (p + 1) * TILE, cols]
            keys = jnp.concatenate([kv_ref[0, pl.ds(a, TILE), cols] for a in starts], axis=0)
            vals = jnp.concatenate([kv_ref[1, pl.ds(a, TILE), cols] for a in starts], axis=0)
            scores = lax.dot_general(
                q, keys, (((1,), (1,)), ((), ())), preferred_element_type=jnp.float32
            ) * HEAD_DIM ** (-0.5)
            slot = lax.broadcasted_iota(jnp.int32, scores.shape, 1) // TILE
            scores = jnp.where(slot < count, scores, jnp.float32(-1e30))
            e = jnp.exp(scores - jnp.max(scores, axis=1, keepdims=True))
            weights = (e / jnp.sum(e, axis=1, keepdims=True)).astype(jnp.bfloat16)
            mixed = jnp.dot(weights, vals, preferred_element_type=jnp.float32)
            out_ref[p * TILE : (p + 1) * TILE, cols] = mixed.astype(jnp.bfloat16)


def shards(ng, nb, nt, tokens, mod_shift, mod_scale, w_qkv, tile_list, tile_count):
    rows, d = tokens.shape
    width = w_qkv.shape[2]
    total = rows * nt
    nc = rows // CHUNK
    chips = nb // 2
    kb = w_qkv.shape[1]
    helped = ng == 2 and chips == 2 and nt == 4 and kb % 64 == 0
    help_rows = 2 * kb if helped else 16
    slots = nt - 2 if helped else 1
    vmem = pl.BlockSpec(memory_space=pltpu.VMEM)
    smem = pl.BlockSpec(memory_space=pltpu.SMEM)
    dma = pltpu.SemaphoreType.DMA
    bf16 = jnp.bfloat16
    q, kv = pl.pallas_call(
        functools.partial(project_kernel, helped, nb, nt),
        out_shape=(
            jax.ShapeDtypeStruct((total, width), bf16),
            jax.ShapeDtypeStruct((2, total + 2 * MARGIN, width), bf16),
        ),
        in_specs=[pl.BlockSpec(memory_space=pl.ANY)] * 4,
        out_specs=(vmem, vmem),
        scratch_shapes=[
            pltpu.VMEM((rows, d), bf16),
            pltpu.VMEM((1, d), jnp.float32),
            pltpu.VMEM((1, d), jnp.float32),
            pltpu.VMEM((total, d), bf16),
            pltpu.VMEM((3, d, width), bf16),
            pltpu.VMEM((3, total + 2 * MARGIN, width), bf16),
            pltpu.VMEM((3, help_rows, width), bf16),
            pltpu.VMEM((slots, 3, rows, width), bf16),
            pltpu.VMEM((slots, 3, rows, width), bf16),
            dma((nt, nc)), dma((nt, nc)), dma((nt, nc)), dma((nt, nc)),
            dma((chips, 3)), dma((chips, 3)), dma((chips, 3)), dma((chips, 3)), dma((3,)),
            dma((nt,)), dma((nt,)), dma((nt,)), dma((nt,)),
            dma((3,)), dma((3,)), dma((3,)), dma((3,)), dma((2, 3)), dma((2, 3)), dma((slots,)), dma((slots,)), dma, dma, dma,
        ],
        compiler_params=pltpu.CompilerParams(
            collective_id=0, has_side_effects=True, vmem_limit_bytes=40 * 2**20
        ),
    )(tokens, mod_shift.reshape(1, d), mod_scale.reshape(1, d), w_qkv)
    return pl.pallas_call(
        attend_kernel,
        out_shape=jax.ShapeDtypeStruct((total, width), bf16),
        in_specs=[smem, smem, vmem, vmem],
        out_specs=vmem,
        compiler_params=pltpu.CompilerParams(vmem_limit_bytes=32 * 2**20),
    )(tile_list, tile_count, q, kv)


def solution(mesh):
    return jax.shard_map(
        functools.partial(shards, mesh.shape["groups"], mesh.shape["block"], mesh.shape["tensor"]),
        mesh=mesh,
        in_specs=(
            P(("groups", "block", "tensor"), None),
            P(),
            P(),
            P(None, "block", "tensor"),
            P(("groups", "block"), None, None),
            P(("groups", "block"), None),
        ),
        out_specs=P(("groups", "block"), "tensor"),
        check_vma=False,
    )
```

```python
import functools

import jax
import jax.numpy as jnp
from jax import lax
from jax.experimental import pallas as pl
from jax.experimental.pallas import tpu as pltpu
from jax.sharding import PartitionSpec as P

HEAD_DIM = 128
TILE = 128
BT = 2
MARGIN = BT * TILE
CHUNK = 32
MESH = pl.DeviceIdType.MESH

epsilon = 1e-06


def project_kernel(
    helped, nb, nt, tokens_hbm, shift_hbm, scale_hbm, w_ref, q_ref, kv_ref,
    tokens_ref, shift_ref, scale_ref, xg, wfull, qkvx, wh, part_out, part_in, up_s, up_r, dn_s, dn_r, wx_s, wx_r, wp_s, wp_r, wl_s,
    hu_s, hu_r, hd_s, hd_r, hz_s, hz_r, hy_s, hy_r, hp_s, hp_r, pt_s, pt_r, tk_s, sh_s, sc_s,
):
    tokens_copy = pltpu.make_async_copy(tokens_hbm, tokens_ref, tk_s)
    tokens_copy.start()
    shift_copy = pltpu.make_async_copy(shift_hbm, shift_ref, sh_s)
    shift_copy.start()
    scale_copy = pltpu.make_async_copy(scale_hbm, scale_ref, sc_s)
    scale_copy.start()
    g = lax.axis_index("groups")
    b = lax.axis_index("block")
    t = lax.axis_index("tensor")
    rows, _ = tokens_ref.shape
    kb = w_ref.shape[1]
    nc = rows // CHUNK
    total = rows * nt
    chips = nb // 2
    chip = b // 2
    core = b % 2
    partner = (g, chip * 2 + (1 - core), t)
    lower = t < nt // 2
    sgn = jnp.where(lower, -1, 1)
    is_end = jnp.logical_or(t == 0, t == nt - 1)
    kc = 2 * kb

    barrier = pltpu.get_barrier_semaphore()
    for j in range(1, nb):
        pl.semaphore_signal(barrier, inc=1, device_id=(g, (b + j) % nb, t), device_id_type=MESH)

    @pl.when(t > 0)
    def _():
        pl.semaphore_signal(barrier, inc=1, device_id=(g, b, t - 1), device_id_type=MESH)

    @pl.when(t < nt - 1)
    def _():
        pl.semaphore_signal(barrier, inc=1, device_id=(g, b, t + 1), device_id_type=MESH)

    if helped:
        pl.semaphore_signal(barrier, inc=1, device_id=(1 - g, b, t), device_id_type=MESH)
    ends = jnp.where(t == 0, 1, 0) + jnp.where(t == nt - 1, 1, 0)
    pl.semaphore_wait(barrier, nb + 1 - ends + (1 if helped else 0))

    def remote(src, dst, s, r, device):
        return pltpu.make_async_remote_copy(
            src_ref=src, dst_ref=dst, send_sem=s, recv_sem=r, device_id=device, device_id_type=MESH
        )

    def w_slab(owner, i):
        return wfull.at[i, pl.ds(pl.multiple_of(owner * kb, 16), kb)]

    def w_cross(j, i, owner, device):
        return remote(w_ref.at[i], w_slab(owner, i), wx_s.at[j, i], wx_r.at[j, i], device)

    def w_pair(j, i, src, owner):
        return remote(src, w_slab(owner, i), wp_s.at[j, i], wp_r.at[j, i], partner)

    for i in range(3):
        for j in range(1, chips):
            w_cross(j, i, b, (g, ((chip + j) % chips) * 2 + core, t)).start()
        w_pair(0, i, w_ref.at[i], b).start()
        pltpu.make_async_copy(w_ref.at[i], w_slab(b, i), wl_s.at[i]).start()

    half = kb // 2

    def h_slab(i, c, part):
        return wh.at[i, pl.ds(pl.multiple_of(c * kb + part * half, 16), half)]

    def h_line(i):
        src = w_ref.at[i, pl.ds(pl.multiple_of(g * half, 16), half)]
        return remote(src, h_slab(i, core, g), hz_s.at[i], hz_r.at[i], (g, b, t - sgn))

    def h_group(i, part):
        slab = h_slab(i, core, part)
        return remote(slab, slab, hy_s.at[i], hy_r.at[i], (1 - g, b, t))

    def h_pair(i, k, c, part):
        slab = h_slab(i, c, part)
        return remote(slab, slab, hp_s.at[k, i], hp_r.at[k, i], partner)

    def x_slab(o, c):
        return xg.at[pl.ds(pl.multiple_of(o * rows + c * CHUNK, 16), CHUNK)]

    def x_half(o, c):
        return xg.at[
            pl.ds(pl.multiple_of(o * rows + c * CHUNK, 16), CHUNK), pl.ds(pl.multiple_of((1 - chip) * kc, 128), kc)
        ]

    def up(s, c, slab=x_slab):
        slab = slab(t - s, c)
        return remote(slab, slab, up_s.at[s, c], up_r.at[s, c], (g, b, t + 1))

    def down(s, c, slab=x_slab):
        slab = slab(t + s, c)
        return remote(slab, slab, dn_s.at[s, c], dn_r.at[s, c], (g, b, t - 1))

    def from_left(s, c, slab=x_slab):
        slab = slab(t - s, c)
        return remote(slab, slab, up_s.at[s - 1, c], up_r.at[s - 1, c], (g, b, t + 1))

    def from_right(s, c, slab=x_slab):
        slab = slab(t + s, c)
        return remote(slab, slab, dn_s.at[s - 1, c], dn_r.at[s - 1, c], (g, b, t - 1))

    def by_width(narrow, act):
        if not helped:
            act(x_slab)
            return

        @pl.when(narrow)
        def _():
            act(x_half)

        @pl.when(jnp.logical_not(narrow))
        def _():
            act(x_slab)

    scale_copy.wait()
    shift_copy.wait()
    tokens_copy.wait()
    gain = 1.0 + scale_ref[...]

    def norm(c, carry):
        x = tokens_ref[pl.ds(pl.multiple_of(c * CHUNK, 16), CHUNK), :].astype(jnp.float32)
        mean = jnp.mean(x, axis=1, keepdims=True)
        x = x - mean
        var = jnp.mean(x * x, axis=1, keepdims=True)
        y = x * lax.rsqrt(var + epsilon) * gain + shift_ref[...]
        xg[pl.ds(pl.multiple_of(t * rows + c * CHUNK, 16), CHUNK), :] = y.astype(jnp.bfloat16)

        @pl.when(t < nt - 1)
        def _():
            up(0, c).start()

        @pl.when(t > 0)
        def _():
            down(0, c).start()

        return carry

    lax.fori_loop(0, nc, norm, 0)
    if helped:

        @pl.when(is_end)
        def _():
            for i in range(3):
                h_line(i).start()


    zeros = jnp.zeros((2, MARGIN, qkvx.shape[2]), qkvx.dtype)

    @pl.when(b == 0)
    def _():
        qkvx[1:3, 0:MARGIN, :] = zeros

    @pl.when(b == nb - 1)
    def _():
        qkvx[1:3, MARGIN + total : 2 * MARGIN + total, :] = zeros

    def relay_left(s, after=None):
        @pl.when(t - s >= 0)
        def _():
            def body(c, carry):
                by_width(jnp.logical_and(t == nt - 1, s >= 2), lambda slab: from_left(s, c, slab).wait_recv())

                @pl.when(t < nt - 1)
                def _():
                    by_width(t == nt - 2, lambda slab: up(s, c, slab).start())

                if after is not None:
                    after(c)
                return carry

            lax.fori_loop(0, nc, body, 0)

    def relay_right(s, after=None):
        @pl.when(t + s < nt)
        def _():
            def body(c, carry):
                by_width(jnp.logical_and(t == 0, s >= 2), lambda slab: from_right(s, c, slab).wait_recv())

                @pl.when(t > 0)
                def _():
                    by_width(t == 1, lambda slab: down(s, c, slab).start())

                if after is not None:
                    after(c)
                return carry

            lax.fori_loop(0, nc, body, 0)

    def relay(s):
        relay_left(s)
        relay_right(s)

    def relay_far(s, after=None):
        @pl.when(lower)
        def _():
            relay_right(s, after)

        @pl.when(jnp.logical_not(lower))
        def _():
            relay_left(s, after)

    def relay_near(s):
        @pl.when(lower)
        def _():
            relay_left(s)

        @pl.when(jnp.logical_not(lower))
        def _():
            relay_right(s)

    def part_send(k):
        return remote(part_out.at[k], part_in.at[k], pt_s.at[k], pt_r.at[k], (g, b, t + sgn))

    def help_end(k):
        o = t - sgn * (k + 1)
        x = xg[pl.ds(pl.multiple_of(o * rows, 16), rows), pl.ds(pl.multiple_of(chip * kc, 128), kc)]

        def one(i, carry):
            y = jnp.dot(x, wh[i], preferred_element_type=jnp.float32)
            part_out[k, i] = y.astype(jnp.bfloat16)
            return carry

        lax.fori_loop(0, 3, one, 0)
        part_send(k).start()

    def halo_up(o):
        return remote(
            qkvx.at[1:3, pl.ds(pl.multiple_of(MARGIN + o * rows, 16), rows)],
            qkvx.at[1:3, pl.ds(pl.multiple_of(o * rows - (total - MARGIN), 16), rows)],
            hu_s.at[o], hu_r.at[o], (g, b + 1, t),
        )

    def halo_down(o):
        return remote(
            qkvx.at[1:3, pl.ds(pl.multiple_of(MARGIN + o * rows, 16), rows)],
            qkvx.at[1:3, pl.ds(pl.multiple_of(MARGIN + total + o * rows, 16), rows)],
            hd_s.at[o], hd_r.at[o], (g, b - 1, t),
        )

    def store(i, o, y):
        qkvx[i, pl.ds(pl.multiple_of(MARGIN + o * rows, 16), rows), :] = y.astype(jnp.bfloat16)

    def whole(o):
        x = xg[pl.ds(pl.multiple_of(o * rows, 16), rows), :]

        def one(i, carry):
            store(i, o, jnp.dot(x, wfull[i], preferred_element_type=jnp.float32))
            return carry

        lax.fori_loop(0, 3, one, 0)

    def rest(o, k):
        other = pl.ds(pl.multiple_of((1 - chip) * kc, 128), kc)
        x = xg[pl.ds(pl.multiple_of(o * rows, 16), rows), other]
        part_send(k).wait_recv()

        def one(i, carry):
            y = jnp.dot(x, wfull[i, other, :], preferred_element_type=jnp.float32)
            store(i, o, y + part_in[k, i].astype(jnp.float32))
            return carry

        lax.fori_loop(0, 3, one, 0)

    def project(o, s):
        if helped:
            narrow = jnp.logical_and(is_end, s >= 2)

            @pl.when(narrow)
            def _():
                rest(o, s - 2)

            @pl.when(jnp.logical_not(narrow))
            def _():
                whole(o)
        else:
            whole(o)

        halos(o)

    def halos(o):
        @pl.when(jnp.logical_and(o * rows >= total - MARGIN, b < nb - 1))
        def _():
            halo_up(o).start()

        @pl.when(jnp.logical_and(o * rows < MARGIN, b > 0))
        def _():
            halo_down(o).start()

    if helped:
        relay_far(1)
        relay_near(1)
    else:
        relay(1)

    for i in range(3):
        for j in range(1, chips):
            owner = ((chip - j + chips) % chips) * 2 + core
            w_cross(j, i, owner, partner).wait_recv()
            w_pair(j, i, w_slab(owner, i), owner).start()

    if helped:

        @pl.when(jnp.logical_not(is_end))
        def _():
            for i in range(3):
                h_line(i).wait_recv()
                h_group(i, g).start()
                h_pair(i, 0, core, g).start()

    for i in range(3):
        pltpu.make_async_copy(w_ref.at[i], w_slab(b, i), wl_s.at[i]).wait()
        for j in range(chips):
            owner = ((chip - j + chips) % chips) * 2 + (1 - core)
            w_pair(j, i, w_slab(owner, i), owner).wait_recv()

    if helped:
        each = -(-6 // nc)

        def between(c):
            def unit(u, carry):
                o = t - sgn * (u // 3)
                i = u % 3
                x = xg[pl.ds(pl.multiple_of(o * rows, 16), rows), :]
                store(i, o, jnp.dot(x, wfull[i], preferred_element_type=jnp.float32))
                return carry

            lax.fori_loop(jnp.minimum(each * c, 6), jnp.minimum(each * (c + 1), 6), unit, 0)

        relay_far(2, between)

        @pl.when(jnp.logical_not(is_end))
        def _():
            for i in range(3):
                h_group(i, 1 - g).wait_recv()
                h_pair(i, 1, core, 1 - g).start()
            for i in range(3):
                h_pair(i, 0, 1 - core, g).wait_recv()
                h_pair(i, 1, 1 - core, 1 - g).wait_recv()

            def assist(k, carry):
                help_end(k)
                return carry

            lax.fori_loop(0, nt - 2, assist, 0)

        halos(t)
        halos(t - sgn)

    def step(s, carry):
        @pl.when(s > (2 if helped else 1))
        def _():
            relay(s)

        def side(d, carry):
            o = t + s * (2 * d - 1)
            todo = jnp.logical_and(o >= 0, o < nt)
            if helped:
                todo = jnp.logical_and(todo, o != t - sgn)

            @pl.when(todo)
            def _():
                project(o, s)

            return carry

        lax.fori_loop(jnp.where(s == 0, 1, 0), 2, side, 0)
        return carry

    lax.fori_loop(1 if helped else 0, nt, step, 0)

    def drain(s, carry):
        def body(c, carry):
            @pl.when(jnp.logical_and(t - s >= 0, t < nt - 1))
            def _():
                by_width(jnp.logical_and(t == nt - 2, s >= 1), lambda slab: up(s, c, slab).wait_send())

            @pl.when(jnp.logical_and(t + s < nt, t > 0))
            def _():
                by_width(jnp.logical_and(t == 1, s >= 1), lambda slab: down(s, c, slab).wait_send())

            return carry

        return lax.fori_loop(0, nc, body, carry)

    lax.fori_loop(0, nt, drain, 0)
    for i in range(3):
        for j in range(1, chips):
            w_cross(j, i, b, partner).wait_send()
        for j in range(chips):
            w_pair(j, i, w_ref.at[i], b).wait_send()

    if helped:

        @pl.when(is_end)
        def _():
            for i in range(3):
                h_line(i).wait_send()

        @pl.when(jnp.logical_not(is_end))
        def _():
            for i in range(3):
                h_group(i, g).wait_send()
                h_pair(i, 0, core, g).wait_send()
                h_pair(i, 1, core, 1 - g).wait_send()
            for k in range(nt - 2):
                part_send(k).wait_send()

    q_ref[...] = qkvx[0, MARGIN : MARGIN + total, :]

    def halo_wait(o, carry):
        @pl.when(o * rows >= total - MARGIN)
        def _():
            @pl.when(b < nb - 1)
            def _():
                halo_up(o).wait_send()

            @pl.when(b > 0)
            def _():
                halo_up(o).wait_recv()

        @pl.when(o * rows < MARGIN)
        def _():
            @pl.when(b > 0)
            def _():
                halo_down(o).wait_send()

            @pl.when(b < nb - 1)
            def _():
                halo_down(o).wait_recv()

        return carry

    lax.fori_loop(0, nt, halo_wait, 0)
    kv_ref[...] = qkvx[1:3]


def attend_kernel(list_ref, count_ref, q_ref, kv_ref, out_ref):
    tiles = q_ref.shape[0] // TILE
    heads = q_ref.shape[1] // HEAD_DIM
    slots = list_ref.shape[2]
    for p in range(tiles):
        count = count_ref[0, p]
        starts = [pl.multiple_of(list_ref[0, p, s] * TILE, TILE) for s in range(slots)]
        for h in range(heads):
            cols = slice(h * HEAD_DIM, (h + 1) * HEAD_DIM)
            q = q_ref[p * TILE : (p + 1) * TILE, cols]
            keys = jnp.concatenate([kv_ref[0, pl.ds(a, TILE), cols] for a in starts], axis=0)
            vals = jnp.concatenate([kv_ref[1, pl.ds(a, TILE), cols] for a in starts], axis=0)
            scores = lax.dot_general(
                q, keys, (((1,), (1,)), ((), ())), preferred_element_type=jnp.float32
            ) * HEAD_DIM ** (-0.5)
            slot = lax.broadcasted_iota(jnp.int32, scores.shape, 1) // TILE
            scores = jnp.where(slot < count, scores, jnp.float32(-1e30))
            e = jnp.exp(scores - jnp.max(scores, axis=1, keepdims=True))
            weights = (e / jnp.sum(e, axis=1, keepdims=True)).astype(jnp.bfloat16)
            mixed = jnp.dot(weights, vals, preferred_element_type=jnp.float32)
            out_ref[p * TILE : (p + 1) * TILE, cols] = mixed.astype(jnp.bfloat16)


def shards(ng, nb, nt, tokens, mod_shift, mod_scale, w_qkv, tile_list, tile_count):
    rows, d = tokens.shape
    width = w_qkv.shape[2]
    total = rows * nt
    nc = rows // CHUNK
    chips = nb // 2
    kb = w_qkv.shape[1]
    helped = ng == 2 and chips == 2 and nt == 4 and kb % 64 == 0
    help_rows = 2 * kb if helped else 16
    slots = nt - 2 if helped else 1
    vmem = pl.BlockSpec(memory_space=pltpu.VMEM)
    smem = pl.BlockSpec(memory_space=pltpu.SMEM)
    dma = pltpu.SemaphoreType.DMA
    bf16 = jnp.bfloat16
    q, kv = pl.pallas_call(
        functools.partial(project_kernel, helped, nb, nt),
        out_shape=(
            jax.ShapeDtypeStruct((total, width), bf16),
            jax.ShapeDtypeStruct((2, total + 2 * MARGIN, width), bf16),
        ),
        in_specs=[pl.BlockSpec(memory_space=pl.ANY)] * 4,
        out_specs=(vmem, vmem),
        scratch_shapes=[
            pltpu.VMEM((rows, d), bf16),
            pltpu.VMEM((1, d), jnp.float32),
            pltpu.VMEM((1, d), jnp.float32),
            pltpu.VMEM((total, d), bf16),
            pltpu.VMEM((3, d, width), bf16),
            pltpu.VMEM((3, total + 2 * MARGIN, width), bf16),
            pltpu.VMEM((3, help_rows, width), bf16),
            pltpu.VMEM((slots, 3, rows, width), bf16),
            pltpu.VMEM((slots, 3, rows, width), bf16),
            dma((nt, nc)), dma((nt, nc)), dma((nt, nc)), dma((nt, nc)),
            dma((chips, 3)), dma((chips, 3)), dma((chips, 3)), dma((chips, 3)), dma((3,)),
            dma((nt,)), dma((nt,)), dma((nt,)), dma((nt,)),
            dma((3,)), dma((3,)), dma((3,)), dma((3,)), dma((2, 3)), dma((2, 3)), dma((slots,)), dma((slots,)), dma, dma, dma,
        ],
        compiler_params=pltpu.CompilerParams(
            collective_id=0, has_side_effects=True, vmem_limit_bytes=60 * 2**20
        ),
    )(tokens, mod_shift.reshape(1, d), mod_scale.reshape(1, d), w_qkv)
    return pl.pallas_call(
        attend_kernel,
        out_shape=jax.ShapeDtypeStruct((total, width), bf16),
        in_specs=[smem, smem, vmem, vmem],
        out_specs=vmem,
        compiler_params=pltpu.CompilerParams(vmem_limit_bytes=32 * 2**20),
    )(tile_list, tile_count, q, kv)


def solution(mesh):
    return jax.shard_map(
        functools.partial(shards, mesh.shape["groups"], mesh.shape["block"], mesh.shape["tensor"]),
        mesh=mesh,
        in_specs=(
            P(("groups", "block", "tensor"), None),
            P(),
            P(),
            P(None, "block", "tensor"),
            P(("groups", "block"), None, None),
            P(("groups", "block"), None),
        ),
        out_specs=P(("groups", "block"), "tensor"),
        check_vma=False,
    )
```

```python
import functools

import jax
import jax.numpy as jnp
from jax import lax
from jax.experimental import pallas as pl
from jax.experimental.pallas import tpu as pltpu
from jax.sharding import PartitionSpec as P

HEAD_DIM = 128
TILE = 128
BT = 2
MARGIN = BT * TILE
CHUNK = 32
MESH = pl.DeviceIdType.MESH

epsilon = 1e-06


def project_kernel(
    helped, nb, nt, tokens_hbm, shift_hbm, scale_hbm, w_ref, q_ref, kv_ref,
    tokens_ref, shift_ref, scale_ref, xg, wfull, qkvx, wh, part_out, part_in, up_s, up_r, dn_s, dn_r, wx_s, wx_r, wp_s, wp_r, wl_s,
    hu_s, hu_r, hd_s, hd_r, hz_s, hz_r, hy_s, hy_r, hp_s, hp_r, pt_s, pt_r, tk_s, sh_s, sc_s,
):
    tokens_copy = pltpu.make_async_copy(tokens_hbm, tokens_ref, tk_s)
    tokens_copy.start()
    shift_copy = pltpu.make_async_copy(shift_hbm, shift_ref, sh_s)
    shift_copy.start()
    scale_copy = pltpu.make_async_copy(scale_hbm, scale_ref, sc_s)
    scale_copy.start()
    g = lax.axis_index("groups")
    b = lax.axis_index("block")
    t = lax.axis_index("tensor")
    rows, _ = tokens_ref.shape
    kb = w_ref.shape[1]
    nc = rows // CHUNK
    total = rows * nt
    chips = nb // 2
    chip = b // 2
    core = b % 2
    partner = (g, chip * 2 + (1 - core), t)
    lower = t < nt // 2
    sgn = jnp.where(lower, -1, 1)
    is_end = jnp.logical_or(t == 0, t == nt - 1)
    kc = 2 * kb

    barrier = pltpu.get_barrier_semaphore()
    for j in range(1, nb):
        pl.semaphore_signal(barrier, inc=1, device_id=(g, (b + j) % nb, t), device_id_type=MESH)

    @pl.when(t > 0)
    def _():
        pl.semaphore_signal(barrier, inc=1, device_id=(g, b, t - 1), device_id_type=MESH)

    @pl.when(t < nt - 1)
    def _():
        pl.semaphore_signal(barrier, inc=1, device_id=(g, b, t + 1), device_id_type=MESH)

    if helped:
        pl.semaphore_signal(barrier, inc=1, device_id=(1 - g, b, t), device_id_type=MESH)
    ends = jnp.where(t == 0, 1, 0) + jnp.where(t == nt - 1, 1, 0)
    pl.semaphore_wait(barrier, nb + 1 - ends + (1 if helped else 0))

    def remote(src, dst, s, r, device):
        return pltpu.make_async_remote_copy(
            src_ref=src, dst_ref=dst, send_sem=s, recv_sem=r, device_id=device, device_id_type=MESH
        )

    def w_slab(owner, i):
        return wfull.at[i, pl.ds(pl.multiple_of(owner * kb, 16), kb)]

    def w_cross(j, i, owner, device):
        return remote(w_ref.at[i], w_slab(owner, i), wx_s.at[j, i], wx_r.at[j, i], device)

    def w_pair(j, i, src, owner):
        return remote(src, w_slab(owner, i), wp_s.at[j, i], wp_r.at[j, i], partner)

    for i in range(3):
        for j in range(1, chips):
            w_cross(j, i, b, (g, ((chip + j) % chips) * 2 + core, t)).start()
        w_pair(0, i, w_ref.at[i], b).start()
        pltpu.make_async_copy(w_ref.at[i], w_slab(b, i), wl_s.at[i]).start()

    half = kb // 2

    def h_slab(i, c, part):
        return wh.at[i, pl.ds(pl.multiple_of(c * kb + part * half, 16), half)]

    def h_line(i):
        src = w_ref.at[i, pl.ds(pl.multiple_of(g * half, 16), half)]
        return remote(src, h_slab(i, core, g), hz_s.at[i], hz_r.at[i], (g, b, t - sgn))

    def h_group(i, part):
        slab = h_slab(i, core, part)
        return remote(slab, slab, hy_s.at[i], hy_r.at[i], (1 - g, b, t))

    def h_pair(i, k, c, part):
        slab = h_slab(i, c, part)
        return remote(slab, slab, hp_s.at[k, i], hp_r.at[k, i], partner)

    if helped:

        @pl.when(is_end)
        def _():
            for i in range(3):
                h_line(i).start()

    def x_slab(o, c):
        return xg.at[pl.ds(pl.multiple_of(o * rows + c * CHUNK, 16), CHUNK)]

    def x_half(o, c):
        return xg.at[
            pl.ds(pl.multiple_of(o * rows + c * CHUNK, 16), CHUNK), pl.ds(pl.multiple_of((1 - chip) * kc, 128), kc)
        ]

    def up(s, c, slab=x_slab):
        slab = slab(t - s, c)
        return remote(slab, slab, up_s.at[s, c], up_r.at[s, c], (g, b, t + 1))

    def down(s, c, slab=x_slab):
        slab = slab(t + s, c)
        return remote(slab, slab, dn_s.at[s, c], dn_r.at[s, c], (g, b, t - 1))

    def from_left(s, c, slab=x_slab):
        slab = slab(t - s, c)
        return remote(slab, slab, up_s.at[s - 1, c], up_r.at[s - 1, c], (g, b, t + 1))

    def from_right(s, c, slab=x_slab):
        slab = slab(t + s, c)
        return remote(slab, slab, dn_s.at[s - 1, c], dn_r.at[s - 1, c], (g, b, t - 1))

    def by_width(narrow, act):
        if not helped:
            act(x_slab)
            return

        @pl.when(narrow)
        def _():
            act(x_half)

        @pl.when(jnp.logical_not(narrow))
        def _():
            act(x_slab)

    scale_copy.wait()
    shift_copy.wait()
    tokens_copy.wait()
    gain = 1.0 + scale_ref[...]

    def norm(c, carry):
        x = tokens_ref[pl.ds(pl.multiple_of(c * CHUNK, 16), CHUNK), :].astype(jnp.float32)
        mean = jnp.mean(x, axis=1, keepdims=True)
        x = x - mean
        var = jnp.mean(x * x, axis=1, keepdims=True)
        y = x * lax.rsqrt(var + epsilon) * gain + shift_ref[...]
        xg[pl.ds(pl.multiple_of(t * rows + c * CHUNK, 16), CHUNK), :] = y.astype(jnp.bfloat16)

        @pl.when(t < nt - 1)
        def _():
            up(0, c).start()

        @pl.when(t > 0)
        def _():
            down(0, c).start()

        return carry

    lax.fori_loop(0, nc, norm, 0)

    zeros = jnp.zeros((2, MARGIN, qkvx.shape[2]), qkvx.dtype)

    @pl.when(b == 0)
    def _():
        qkvx[1:3, 0:MARGIN, :] = zeros

    @pl.when(b == nb - 1)
    def _():
        qkvx[1:3, MARGIN + total : 2 * MARGIN + total, :] = zeros

    def relay_left(s):
        @pl.when(t - s >= 0)
        def _():
            def body(c, carry):
                by_width(jnp.logical_and(t == nt - 1, s >= 2), lambda slab: from_left(s, c, slab).wait_recv())

                @pl.when(t < nt - 1)
                def _():
                    by_width(t == nt - 2, lambda slab: up(s, c, slab).start())

                return carry

            lax.fori_loop(0, nc, body, 0)

    def relay_right(s):
        @pl.when(t + s < nt)
        def _():
            def body(c, carry):
                by_width(jnp.logical_and(t == 0, s >= 2), lambda slab: from_right(s, c, slab).wait_recv())

                @pl.when(t > 0)
                def _():
                    by_width(t == 1, lambda slab: down(s, c, slab).start())

                return carry

            lax.fori_loop(0, nc, body, 0)

    def relay(s):
        relay_left(s)
        relay_right(s)

    def relay_far(s):
        @pl.when(lower)
        def _():
            relay_right(s)

        @pl.when(jnp.logical_not(lower))
        def _():
            relay_left(s)

    def relay_near(s):
        @pl.when(lower)
        def _():
            relay_left(s)

        @pl.when(jnp.logical_not(lower))
        def _():
            relay_right(s)

    def part_send(k):
        return remote(part_out.at[k], part_in.at[k], pt_s.at[k], pt_r.at[k], (g, b, t + sgn))

    def help_end(k):
        o = t - sgn * (k + 1)
        x = xg[pl.ds(pl.multiple_of(o * rows, 16), rows), pl.ds(pl.multiple_of(chip * kc, 128), kc)]

        def one(i, carry):
            y = jnp.dot(x, wh[i], preferred_element_type=jnp.float32)
            part_out[k, i] = y.astype(jnp.bfloat16)
            return carry

        lax.fori_loop(0, 3, one, 0)
        part_send(k).start()

    def halo_up(o):
        return remote(
            qkvx.at[1:3, pl.ds(pl.multiple_of(MARGIN + o * rows, 16), rows)],
            qkvx.at[1:3, pl.ds(pl.multiple_of(o * rows - (total - MARGIN), 16), rows)],
            hu_s.at[o], hu_r.at[o], (g, b + 1, t),
        )

    def halo_down(o):
        return remote(
            qkvx.at[1:3, pl.ds(pl.multiple_of(MARGIN + o * rows, 16), rows)],
            qkvx.at[1:3, pl.ds(pl.multiple_of(MARGIN + total + o * rows, 16), rows)],
            hd_s.at[o], hd_r.at[o], (g, b - 1, t),
        )

    def store(i, o, y):
        qkvx[i, pl.ds(pl.multiple_of(MARGIN + o * rows, 16), rows), :] = y.astype(jnp.bfloat16)

    def whole(o):
        x = xg[pl.ds(pl.multiple_of(o * rows, 16), rows), :]

        def one(i, carry):
            store(i, o, jnp.dot(x, wfull[i], preferred_element_type=jnp.float32))
            return carry

        lax.fori_loop(0, 3, one, 0)

    def rest(o, k):
        other = pl.ds(pl.multiple_of((1 - chip) * kc, 128), kc)
        x = xg[pl.ds(pl.multiple_of(o * rows, 16), rows), other]
        part_send(k).wait_recv()

        def one(i, carry):
            y = jnp.dot(x, wfull[i, other, :], preferred_element_type=jnp.float32)
            store(i, o, y + part_in[k, i].astype(jnp.float32))
            return carry

        lax.fori_loop(0, 3, one, 0)

    def project(o, s):
        if helped:
            narrow = jnp.logical_and(is_end, s >= 2)

            @pl.when(narrow)
            def _():
                rest(o, s - 2)

            @pl.when(jnp.logical_not(narrow))
            def _():
                whole(o)
        else:
            whole(o)

        @pl.when(jnp.logical_and(o * rows >= total - MARGIN, b < nb - 1))
        def _():
            halo_up(o).start()

        @pl.when(jnp.logical_and(o * rows < MARGIN, b > 0))
        def _():
            halo_down(o).start()

    if helped:
        relay_far(1)

        @pl.when(jnp.logical_not(is_end))
        def _():
            for i in range(3):
                h_line(i).wait_recv()
                h_group(i, g).start()
                h_pair(i, 0, core, g).start()

        relay_near(1)
    else:
        relay(1)

    for i in range(3):
        for j in range(1, chips):
            owner = ((chip - j + chips) % chips) * 2 + core
            w_cross(j, i, owner, partner).wait_recv()
            w_pair(j, i, w_slab(owner, i), owner).start()

    if helped:

        @pl.when(jnp.logical_not(is_end))
        def _():
            for i in range(3):
                h_group(i, 1 - g).wait_recv()
                h_pair(i, 1, core, 1 - g).start()

        relay_far(2)

        @pl.when(jnp.logical_not(is_end))
        def _():
            for i in range(3):
                h_pair(i, 0, 1 - core, g).wait_recv()
                h_pair(i, 1, 1 - core, 1 - g).wait_recv()

            def assist(k, carry):
                help_end(k)
                return carry

            lax.fori_loop(0, nt - 2, assist, 0)

    for i in range(3):
        pltpu.make_async_copy(w_ref.at[i], w_slab(b, i), wl_s.at[i]).wait()
        for j in range(chips):
            owner = ((chip - j + chips) % chips) * 2 + (1 - core)
            w_pair(j, i, w_slab(owner, i), owner).wait_recv()

    def step(s, carry):
        @pl.when(s > (2 if helped else 1))
        def _():
            relay(s)

        def side(d, carry):
            o = t + s * (2 * d - 1)

            @pl.when(jnp.logical_and(o >= 0, o < nt))
            def _():
                project(o, s)

            return carry

        lax.fori_loop(jnp.where(s == 0, 1, 0), 2, side, 0)
        return carry

    lax.fori_loop(0, nt, step, 0)

    def drain(s, carry):
        def body(c, carry):
            @pl.when(jnp.logical_and(t - s >= 0, t < nt - 1))
            def _():
                by_width(jnp.logical_and(t == nt - 2, s >= 1), lambda slab: up(s, c, slab).wait_send())

            @pl.when(jnp.logical_and(t + s < nt, t > 0))
            def _():
                by_width(jnp.logical_and(t == 1, s >= 1), lambda slab: down(s, c, slab).wait_send())

            return carry

        return lax.fori_loop(0, nc, body, carry)

    lax.fori_loop(0, nt, drain, 0)
    for i in range(3):
        for j in range(1, chips):
            w_cross(j, i, b, partner).wait_send()
        for j in range(chips):
            w_pair(j, i, w_ref.at[i], b).wait_send()

    if helped:

        @pl.when(is_end)
        def _():
            for i in range(3):
                h_line(i).wait_send()

        @pl.when(jnp.logical_not(is_end))
        def _():
            for i in range(3):
                h_group(i, g).wait_send()
                h_pair(i, 0, core, g).wait_send()
                h_pair(i, 1, core, 1 - g).wait_send()
            for k in range(nt - 2):
                part_send(k).wait_send()

    q_ref[...] = qkvx[0, MARGIN : MARGIN + total, :]

    def halo_wait(o, carry):
        @pl.when(o * rows >= total - MARGIN)
        def _():
            @pl.when(b < nb - 1)
            def _():
                halo_up(o).wait_send()

            @pl.when(b > 0)
            def _():
                halo_up(o).wait_recv()

        @pl.when(o * rows < MARGIN)
        def _():
            @pl.when(b > 0)
            def _():
                halo_down(o).wait_send()

            @pl.when(b < nb - 1)
            def _():
                halo_down(o).wait_recv()

        return carry

    lax.fori_loop(0, nt, halo_wait, 0)
    kv_ref[...] = qkvx[1:3]


def attend_kernel(list_ref, count_ref, q_ref, kv_ref, out_ref):
    tiles = q_ref.shape[0] // TILE
    heads = q_ref.shape[1] // HEAD_DIM
    slots = list_ref.shape[2]
    for p in range(tiles):
        count = count_ref[0, p]
        starts = [pl.multiple_of(list_ref[0, p, s] * TILE, TILE) for s in range(slots)]
        for h in range(heads):
            cols = slice(h * HEAD_DIM, (h + 1) * HEAD_DIM)
            q = q_ref[p * TILE : (p + 1) * TILE, cols]
            keys = jnp.concatenate([kv_ref[0, pl.ds(a, TILE), cols] for a in starts], axis=0)
            vals = jnp.concatenate([kv_ref[1, pl.ds(a, TILE), cols] for a in starts], axis=0)
            scores = lax.dot_general(
                q, keys, (((1,), (1,)), ((), ())), preferred_element_type=jnp.float32
            ) * HEAD_DIM ** (-0.5)
            slot = lax.broadcasted_iota(jnp.int32, scores.shape, 1) // TILE
            scores = jnp.where(slot < count, scores, jnp.float32(-1e30))
            e = jnp.exp(scores - jnp.max(scores, axis=1, keepdims=True))
            weights = (e / jnp.sum(e, axis=1, keepdims=True)).astype(jnp.bfloat16)
            mixed = jnp.dot(weights, vals, preferred_element_type=jnp.float32)
            out_ref[p * TILE : (p + 1) * TILE, cols] = mixed.astype(jnp.bfloat16)


def shards(ng, nb, nt, tokens, mod_shift, mod_scale, w_qkv, tile_list, tile_count):
    rows, d = tokens.shape
    width = w_qkv.shape[2]
    total = rows * nt
    nc = rows // CHUNK
    chips = nb // 2
    kb = w_qkv.shape[1]
    helped = ng == 2 and chips == 2 and nt == 4 and kb % 64 == 0
    help_rows = 2 * kb if helped else 16
    slots = nt - 2 if helped else 1
    vmem = pl.BlockSpec(memory_space=pltpu.VMEM)
    smem = pl.BlockSpec(memory_space=pltpu.SMEM)
    dma = pltpu.SemaphoreType.DMA
    bf16 = jnp.bfloat16
    q, kv = pl.pallas_call(
        functools.partial(project_kernel, helped, nb, nt),
        out_shape=(
            jax.ShapeDtypeStruct((total, width), bf16),
            jax.ShapeDtypeStruct((2, total + 2 * MARGIN, width), bf16),
        ),
        in_specs=[pl.BlockSpec(memory_space=pl.ANY)] * 4,
        out_specs=(vmem, vmem),
        scratch_shapes=[
            pltpu.VMEM((rows, d), bf16),
            pltpu.VMEM((1, d), jnp.float32),
            pltpu.VMEM((1, d), jnp.float32),
            pltpu.VMEM((total, d), bf16),
            pltpu.VMEM((3, d, width), bf16),
            pltpu.VMEM((3, total + 2 * MARGIN, width), bf16),
            pltpu.VMEM((3, help_rows, width), bf16),
            pltpu.VMEM((slots, 3, rows, width), bf16),
            pltpu.VMEM((slots, 3, rows, width), bf16),
            dma((nt, nc)), dma((nt, nc)), dma((nt, nc)), dma((nt, nc)),
            dma((chips, 3)), dma((chips, 3)), dma((chips, 3)), dma((chips, 3)), dma((3,)),
            dma((nt,)), dma((nt,)), dma((nt,)), dma((nt,)),
            dma((3,)), dma((3,)), dma((3,)), dma((3,)), dma((2, 3)), dma((2, 3)), dma((slots,)), dma((slots,)), dma, dma, dma,
        ],
        compiler_params=pltpu.CompilerParams(
            collective_id=0, has_side_effects=True, vmem_limit_bytes=60 * 2**20
        ),
    )(tokens, mod_shift.reshape(1, d), mod_scale.reshape(1, d), w_qkv)
    return pl.pallas_call(
        attend_kernel,
        out_shape=jax.ShapeDtypeStruct((total, width), bf16),
        in_specs=[smem, smem, vmem, vmem],
        out_specs=vmem,
        compiler_params=pltpu.CompilerParams(vmem_limit_bytes=32 * 2**20),
    )(tile_list, tile_count, q, kv)


def solution(mesh):
    return jax.shard_map(
        functools.partial(shards, mesh.shape["groups"], mesh.shape["block"], mesh.shape["tensor"]),
        mesh=mesh,
        in_specs=(
            P(("groups", "block", "tensor"), None),
            P(),
            P(),
            P(None, "block", "tensor"),
            P(("groups", "block"), None, None),
            P(("groups", "block"), None),
        ),
        out_specs=P(("groups", "block"), "tensor"),
        check_vma=False,
    )
```
